32 devices in a mesh: pole: 2 (over x), row: 16 (over z, y, core).
Axes of the slice: x: 2, y: 2, z: 4, core: 2. Of those that a mesh axis runs over, the one named last changes fastest.
Arguments:
- anc_inv: bfloat16 [4096, 2048], P(('pole', 'row')), parts along dimension 0, as said below
- lower_one: bfloat16 [4096, 768], P(('pole', 'row')), parts along dimension 0, may hold values from -0.125 to 0.125
- pattern_one: int32 [16, 6], P('row'), may hold values from 0 to 1
- pivot_one: float32 [1536, 128], P('pole'), parts along dimension 0, as said below
- lower_zero: bfloat16 [4096, 512], P(('pole', 'row')), parts along dimension 0, may hold values from -0.125 to 0.125
- pattern_zero: int32 [16, 4], P('row'), may hold values from 0 to 1
- coupling_zero: bfloat16 [1536, 512], P('pole'), parts along dimension 0, may hold values from -0.21875 to 0.21875
- pattern_couple: int32 [6, 4], replicated, may hold values from 0 to 1
- pivot_zero: float32 [1024, 128], P('pole'), parts along dimension 0, as said below
Outputs:
- inv_cross: bfloat16 [4096, 768], P(('pole', 'row')), parts along dimension 0
- inv_pivot: float32 [1536, 768], P('pole'), parts along dimension 0
- inv_low: bfloat16 [4096, 512], P(('pole', 'row')), parts along dimension 0
- inv_couple: float32 [1536, 512], P('pole'), parts along dimension 0
- inv_diag: float32 [1024, 512], P('pole'), parts along dimension 0
The draws below stay inside these ranges and needn't reach their ends.
There are 2 independent parts, one for each index of `pole`. The reference program is written for one: setup_inputs(seed, part) draws one part's arguments, and reference() takes and returns one part's arrays. A program takes and returns all parts, laid end to end along the dimension named above; an argument that names none is the same for every part. Nothing has to cross between parts.
Inputs may be any that keep to these rules, and one draw needn't show every extreme that they name: anc_inv equals its transpose. Each stacked block of pivot_one equals its transpose. Each stacked block of pivot_zero equals its transpose.
All inputs are finite; a program needn't handle non-finite values.
Results may differ from the reference program's by a relative error of at most 0.0037.
Values may be sent and summed in bfloat16 or wider, within the bound.
A program may use at most 128 MiB of HBM per device.

```python
import math
import jax
import jax.numpy as jnp
from jax import lax

B = 128
K1 = 6
K0 = 4
NC = 16


def symmetric_blocks(key, count, size):
    base = jax.random.normal(key, (count, size, size), jnp.float32)
    sym = (base + jnp.swapaxes(base, 1, 2)) * (0.5 / math.sqrt(size))
    return (sym + 2.0 * jnp.eye(size, dtype=jnp.float32)[None]).reshape(count * size, size)


def block_pattern(key, rows, cols):
    thresh = 20 + 70 * jnp.arange(rows, dtype=jnp.int32) // max(rows - 1, 1)
    picks = jax.random.randint(key, (rows, cols), 0, 100)
    return (picks < thresh[:, None]).astype(jnp.int32)


def draw_anc_inv(key, part):
    key = jax.random.fold_in(key, 11)
    order = NC * B
    first = jax.random.fold_in(key, 0)
    base = jax.random.normal(first, (order, order), jnp.float32)
    sym = (base + base.T) * (0.5 / math.sqrt(order))
    sym = sym + jnp.diag(jnp.ones((order,), jnp.float32))
    return sym.astype(jnp.bfloat16)


def draw_pivot_one(key, part):
    key = jax.random.fold_in(key, 13)
    return symmetric_blocks(key, K1, B)


def draw_pivot_zero(key, part):
    key = jax.random.fold_in(key, 17)
    return symmetric_blocks(key, K0, B)


def draw_pattern_one(key, part):
    key = jax.random.fold_in(key, 21)
    return block_pattern(key, NC, K1)


def draw_pattern_zero(key, part):
    key = jax.random.fold_in(key, 23)
    return block_pattern(key, NC, K0)


def draw_pattern_couple(key, part):
    key = jax.random.fold_in(key, 29)
    return block_pattern(key, K1, K0)


def block_scale(rng, shape, cuts, least, top_value):
    gain = 1.0
    for dim, blocks in cuts:
        draws = jax.random.uniform(jax.random.fold_in(jax.random.fold_in(rng, 6), dim), (blocks,), jnp.float32, least / len(cuts), top_value / len(cuts))
        gain = gain * jnp.repeat(jnp.exp(draws), shape[dim] // blocks).reshape((-1,) + (1,) * (len(shape) - 1 - dim))
    return gain


def bell_draw(rng, extent, deviation, most, pieces=(), kind=jnp.bfloat16):
    entries = deviation * jax.random.normal(rng, extent, jnp.float32)
    if pieces:
        entries = entries * block_scale(rng, extent, pieces, -0.22, 0.18)
    return jnp.clip(entries, -most, most).astype(kind)


def setup_inputs(seed: int = 0, part: int = 0) -> dict:
    streams_of = jax.random.split(jax.random.key(seed), 10)
    part_splits = jax.random.split(jax.random.fold_in(streams_of[9], part), 10)
    return {
        "anc_inv": draw_anc_inv(jax.random.fold_in(jax.random.fold_in(streams_of[9], part), 71), part),
        "lower_one": bell_draw(part_splits[1], (NC * B, K1 * B), (NC * B) ** -0.5, 0.125, ((0, 16),)),
        "pattern_one": draw_pattern_one(jax.random.fold_in(streams_of[9], 71), part),
        "pivot_one": draw_pivot_one(jax.random.fold_in(jax.random.fold_in(streams_of[9], part), 71), part),
        "lower_zero": bell_draw(part_splits[4], (NC * B, K0 * B), (NC * B) ** -0.5, 0.125, ((0, 16),)),
        "pattern_zero": draw_pattern_zero(jax.random.fold_in(streams_of[9], 71), part),
        "coupling_zero": bell_draw(part_splits[6], (K1 * B, K0 * B), (K1 * B) ** -0.5, 0.21875),
        "pattern_couple": draw_pattern_couple(jax.random.fold_in(streams_of[9], 71), part),
        "pivot_zero": draw_pivot_zero(jax.random.fold_in(jax.random.fold_in(streams_of[9], part), 71), part),
    }


def masked(values, pattern):
    rows, cols = pattern.shape
    size = values.shape[0] // rows
    blocks = values.reshape(rows, size, cols, size) * pattern[:, None, :, None].astype(values.dtype)
    return blocks.reshape(rows * size, cols * size)


def add_blocks(matrix, stacked):
    size = stacked.shape[1]
    count = stacked.shape[0] // size
    eye_k = jnp.eye(count, dtype=jnp.float32)
    placed = stacked.reshape(count, size, size)[:, :, None, :] * eye_k[:, None, :, None]
    return matrix + placed.reshape(count * size, count * size)


def reference(anc_inv, lower_one, pattern_one, pivot_one, lower_zero, pattern_zero, coupling_zero, pattern_couple, pivot_zero):
    upper = masked(lower_one, pattern_one)
    lower = masked(lower_zero, pattern_zero)
    coupling = masked(coupling_zero, pattern_couple)
    inv_cross = (-jnp.dot(anc_inv, upper, preferred_element_type=jnp.float32)).astype(jnp.bfloat16)
    inv_pivot = add_blocks(-jnp.dot(upper.T, inv_cross, preferred_element_type=jnp.float32), pivot_one)
    pivot_b = inv_pivot.astype(jnp.bfloat16)
    low_sum = jnp.dot(anc_inv, lower, preferred_element_type=jnp.float32) + jnp.dot(inv_cross, coupling, preferred_element_type=jnp.float32)
    inv_low = (-low_sum).astype(jnp.bfloat16)
    inv_couple = -(jnp.dot(inv_cross.T, lower, preferred_element_type=jnp.float32) + jnp.dot(pivot_b, coupling, preferred_element_type=jnp.float32))
    diag_update = jnp.dot(lower.T, inv_low, preferred_element_type=jnp.float32)
    diag_update = diag_update + jnp.dot(coupling.astype(jnp.float32).T, inv_couple, precision=lax.Precision.HIGHEST)
    inv_diag = add_blocks(-diag_update, pivot_zero)
    return inv_cross, inv_pivot, inv_low, inv_couple, inv_diag
```

```python
import functools

import jax
import jax.numpy as jnp
from jax import lax
from jax.experimental import pallas as pl
from jax.experimental.pallas import tpu as pltpu
from jax.sharding import PartitionSpec as P

F32 = jnp.float32
BF16 = jnp.bfloat16
MESH = pl.DeviceIdType.MESH


def mul(a, b):
    return jnp.dot(a, b, preferred_element_type=F32)


def mul_t(a, b):
    return lax.dot_general(a, b, (((0,), (0,)), ((), ())), preferred_element_type=F32)


def kernel(
    n, snake, k1, k0, size,
    anc, l_one, pat_one, piv_one, l_zero, pat_zero, couple, pat_couple, piv_zero,
    o_cross, o_pivot, o_low, o_couple, o_diag,
    up, lo, x_up, x_lo, part, sib_part, half, from_left, from_right, out_left, out_right, total,
    ag_send, ag_recv, sib_send, sib_recv, pair_send, pair_recv,
    rs_send, rs_recv, fin_send, fin_recv, fs_send, fs_recv,
):
    chips = n // 2
    far = chips // 2
    blocks = k1 + k0
    rows = size
    me = lax.axis_index("row")
    core = me % 2
    chip = me // 2

    def chip_at(q):
        q = (q + chips) % chips
        if not snake:
            return q
        h = q // far
        return (1 - h) * 2 * q + h * (2 * (chips - 1 - q) + 1)

    if snake:
        y = chip % 2
        z = chip // 2
        pos = z * (1 - y) + (chips - 1 - z) * y
    else:
        pos = chip
    right = chip_at(pos + 1) * 2 + core
    left = chip_at(pos - 1) * 2 + core
    sib = chip * 2 + (1 - core)

    barrier = pltpu.get_barrier_semaphore()
    for other in (left, right, sib):
        pl.semaphore_signal(barrier, inc=1, device_id={"row": other}, device_id_type=MESH)

    own = pl.ds(pl.multiple_of(me * rows, rows), rows)
    for j in range(k1):
        cols = slice(j * size, (j + 1) * size)
        up[own, cols] = (l_one[:, cols].astype(F32) * pat_one[0, j].astype(F32)).astype(BF16)
    for j in range(k0):
        cols = slice(j * size, (j + 1) * size)
        lo[own, cols] = (l_zero[:, cols].astype(F32) * pat_zero[0, j].astype(F32)).astype(BF16)
    pl.semaphore_wait(barrier, 3)

    bufs = (up, lo)

    def copy(src, dst, ss, rs, target):
        return pltpu.make_async_remote_copy(
            src_ref=src, dst_ref=dst, send_sem=ss, recv_sem=rs,
            device_id={"row": target}, device_id_type=MESH)

    pending = []

    def block(ch, q, kk):
        r = chip_at(q) * 2 + kk
        return bufs[ch].at[pl.ds(pl.multiple_of(r * rows, rows), rows), :]

    def origin(d, s):
        return pos - s if d == 0 else pos + s

    def ring(d, s, ch, q):
        ref = block(ch, q, core)
        return copy(ref, ref, ag_send.at[d, s, ch], ag_recv.at[d, s, ch], right if d == 0 else left)

    def pair(d, s, ch, kk):
        ref = block(ch, origin(d, s), kk)
        return copy(ref, ref, sib_send.at[d, s, ch], sib_recv.at[d, s, ch], sib)

    def active(d, s, ch):
        return s < far or (s == far and ch == d)

    def start(c):
        c.start()
        pending.append(c)

    for ch in range(2):
        for d in range(2):
            if active(d, 1, ch):
                start(ring(d, 1, ch, pos))
    for ch in range(2):
        start(pair(0, 0, ch, core))

    def add(ch, q, first=False):
        c = chip_at(q)
        cols = pl.ds(pl.multiple_of(c * 2 * rows, 2 * rows), 2 * rows)
        acc = (x_up, x_lo)[ch]
        term = mul(anc[:, cols], bufs[ch][cols, :])
        if first:
            acc[...] = term
        else:
            acc[...] += term

    def settle(s):
        for ch in range(2):
            for d in range(2):
                if (s == 0 and d == 0) or (s > 0 and active(d, s, ch)):
                    pair(d, s, ch, 1 - core).wait_recv()
                    add(ch, origin(d, s), s == 0)

    for s in range(1, far + 1):
        for ch in range(2):
            for d in range(2):
                if active(d, s, ch):
                    ring(d, s, ch, origin(d, s)).wait_recv()
                    if active(d, s + 1, ch):
                        start(ring(d, s + 1, ch, origin(d, s)))
                    start(pair(d, s, ch, core))
        settle(s - 1)
    settle(far)

    xb_up = x_up[...].astype(BF16)
    xb_lo = x_lo[...].astype(BF16)
    o_cross[...] = -xb_up
    own_l = jnp.concatenate([up[own, :], lo[own, :]], axis=1)
    xb = jnp.concatenate([xb_up, xb_lo], axis=1)

    where = {}
    at = 0
    for i in range(blocks):
        g = mul_t(xb[:, i * size:(i + 1) * size], own_l[:, i * size:])
        for j in range(i, blocks):
            where[i, j] = at
            part[at * size:(at + 1) * size, :] = g[:, (j - i) * size:(j - i + 1) * size].astype(BF16)
            at += 1
    packed = part.shape[0]
    if at * size < packed:
        part[at * size:, :] = jnp.zeros((packed - at * size, size), BF16)
    hrows = packed // 2
    piece = hrows // chips

    def half_at(kk):
        return pl.ds(pl.multiple_of(kk * hrows, hrows), hrows)

    swap = copy(part.at[half_at(1 - core), :], sib_part, pair_send, pair_recv, sib)
    start(swap)

    lk = [[None] * k0 for _ in range(k1)]
    for i in range(k1):
        for j in range(k0):
            lk[i][j] = (couple[i * size:(i + 1) * size, j * size:(j + 1) * size].astype(F32)
                        * pat_couple[i, j].astype(F32)).astype(BF16)
    lkm = jnp.concatenate([jnp.concatenate(r, axis=1) for r in lk], axis=0)
    o_low[...] = (-(x_lo[...] - mul(xb_up, lkm))).astype(BF16)

    swap.wait_recv()
    half[...] = part[half_at(core), :].astype(F32) + sib_part[...].astype(F32)

    def of_piece(q):
        q = (q + chips) % chips
        return pl.ds(pl.multiple_of(q * piece, piece), piece)

    outs = (out_right, out_left)
    ins = (from_left, from_right)
    reach = (far, chips - 1 - far)

    def rs(d, s):
        return copy(outs[d].at[s - 1], ins[d].at[s - 1], rs_send.at[d, s], rs_recv.at[d, s],
                    right if d == 0 else left)

    for s in range(1, far + 1):
        for d in range(2):
            if s > reach[d]:
                continue
            q = pos + (reach[d] - s + 1) * (1 if d == 0 else -1)
            value = half[of_piece(q), :]
            if s > 1:
                rs(d, s - 1).wait_recv()
                value = value + ins[d][s - 2].astype(F32)
            outs[d][s - 1] = value.astype(BF16)
            start(rs(d, s))
    value = half[of_piece(pos), :]
    for d in range(2):
        rs(d, reach[d]).wait_recv()
        value = value + ins[d][reach[d] - 1].astype(F32)
    cut = (piece // 32) * 16
    spans = ((0, cut), (cut, piece - cut))
    total[pl.ds(pl.multiple_of(core * hrows + pos * piece, 16), piece), :] = value.astype(BF16)

    def fin_block(ch, q, kk):
        q = (q + chips) % chips
        off, count = spans[ch]
        return total.at[pl.ds(pl.multiple_of(kk * hrows + q * piece + off, 16), count), :]

    def fin(d, s, ch, q):
        ref = fin_block(ch, q, core)
        return copy(ref, ref, fin_send.at[d, s, ch], fin_recv.at[d, s, ch], right if d == 0 else left)

    def fin_pair(d, s, ch, kk):
        ref = fin_block(ch, origin(d, s), kk)
        return copy(ref, ref, fs_send.at[d, s, ch], fs_recv.at[d, s, ch], sib)

    for ch in range(2):
        for d in range(2):
            if active(d, 1, ch):
                start(fin(d, 1, ch, pos))
    for ch in range(2):
        start(fin_pair(0, 0, ch, core))
    for s in range(1, far + 1):
        for ch in range(2):
            for d in range(2):
                if active(d, s, ch):
                    fin(d, s, ch, origin(d, s)).wait_recv()
                    if active(d, s + 1, ch):
                        start(fin(d, s + 1, ch, origin(d, s)))
                    start(fin_pair(d, s, ch, core))
    for s in range(far + 1):
        for ch in range(2):
            for d in range(2):
                if (s == 0 and d == 0) or (s > 0 and active(d, s, ch)):
                    fin_pair(d, s, ch, 1 - core).wait_recv()

    def tri(i, j):
        b = where[i, j]
        return total[b * size:(b + 1) * size, :].astype(F32)

    for i in range(k1):
        for j in range(i, k1):
            g = tri(i, j)
            ri, rj = slice(i * size, (i + 1) * size), slice(j * size, (j + 1) * size)
            if i == j:
                o_pivot[ri, rj] = g + piv_one[ri, :]
            else:
                o_pivot[ri, rj] = g
                o_pivot[rj, ri] = g.T
    pivot_b = o_pivot[...].astype(BF16)
    cross = jnp.concatenate(
        [jnp.concatenate([total[where[i, k1 + j] * size:(where[i, k1 + j] + 1) * size, :] for j in range(k0)], axis=1)
         for i in range(k1)], axis=0)
    coupled = cross.astype(F32) - mul(pivot_b, lkm)
    o_couple[...] = coupled
    high = coupled.astype(BF16)
    low = (coupled - high.astype(F32)).astype(BF16)
    update = mul_t(cross, lkm) + mul_t(lkm, high) + mul_t(lkm, low)
    for i in range(k0):
        for j in range(i, k0):
            g = tri(k1 + i, k1 + j)
            ri, rj = slice(i * size, (i + 1) * size), slice(j * size, (j + 1) * size)
            if i == j:
                o_diag[ri, rj] = g + piv_zero[ri, :] - update[ri, rj]
            else:
                o_diag[ri, rj] = g - update[ri, rj]
                o_diag[rj, ri] = g.T - update[rj, ri]

    for c in pending:
        c.wait_send()


def per_device(n, snake, *args):
    anc, l_one, pat_one, piv_one, l_zero, pat_zero, couple, pat_couple, piv_zero = args
    rows, order = anc.shape
    size = piv_one.shape[1]
    w1, w0 = l_one.shape[1], l_zero.shape[1]
    k1, k0 = w1 // size, w0 // size
    blocks = k1 + k0
    tri = blocks * (blocks + 1) // 2 * size
    unit = 16 * n
    packed = -(-tri // unit) * unit
    chips = n // 2
    far = chips // 2
    piece = packed // n
    vmem = pl.BlockSpec(memory_space=pltpu.VMEM)
    smem = pl.BlockSpec(memory_space=pltpu.SMEM)
    dma = pltpu.SemaphoreType.DMA
    return pl.pallas_call(
        functools.partial(kernel, n, snake, k1, k0, size),
        out_shape=(
            jax.ShapeDtypeStruct((rows, w1), BF16),
            jax.ShapeDtypeStruct((w1, w1), F32),
            jax.ShapeDtypeStruct((rows, w0), BF16),
            jax.ShapeDtypeStruct((w1, w0), F32),
            jax.ShapeDtypeStruct((w0, w0), F32),
        ),
        in_specs=[vmem, vmem, smem, vmem, vmem, smem, vmem, smem, vmem],
        out_specs=(vmem,) * 5,
        scratch_shapes=[
            pltpu.VMEM((order, w1), BF16),
            pltpu.VMEM((order, w0), BF16),
            pltpu.VMEM((rows, w1), F32),
            pltpu.VMEM((rows, w0), F32),
            pltpu.VMEM((packed, size), BF16),
            pltpu.VMEM((packed // 2, size), BF16),
            pltpu.VMEM((packed // 2, size), F32),
            pltpu.VMEM((far, piece, size), BF16),
            pltpu.VMEM((far, piece, size), BF16),
            pltpu.VMEM((far, piece, size), BF16),
            pltpu.VMEM((far, piece, size), BF16),
            pltpu.VMEM((packed, size), BF16),
            dma((2, far + 1, 2)), dma((2, far + 1, 2)),
            dma((2, far + 1, 2)), dma((2, far + 1, 2)),
            dma, dma,
            dma((2, far + 1)), dma((2, far + 1)),
            dma((2, far + 1, 2)), dma((2, far + 1, 2)),
            dma((2, far + 1, 2)), dma((2, far + 1, 2)),
        ],
        compiler_params=pltpu.CompilerParams(
            collective_id=0, has_side_effects=True, vmem_limit_bytes=56 * 1024 * 1024),
    )(*args)


def solution(mesh):
    n = mesh.shape["row"]
    placed = (
        P(("pole", "row"), None),
        P(("pole", "row"), None),
        P("row", None),
        P("pole", None),
        P(("pole", "row"), None),
        P("row", None),
        P("pole", None),
        P(),
        P("pole", None),
    )
    return jax.shard_map(
        functools.partial(per_device, n, n == 16),
        mesh=mesh,
        in_specs=placed,
        out_specs=(
            P(("pole", "row"), None),
            P("pole", None),
            P(("pole", "row"), None),
            P("pole", None),
            P("pole", None),
        ),
        check_vma=False,
    )
```

```python
import functools

import jax
import jax.numpy as jnp
from jax import lax
from jax.experimental import pallas as pl
from jax.experimental.pallas import tpu as pltpu
from jax.sharding import PartitionSpec as P

F32 = jnp.float32
BF16 = jnp.bfloat16
MESH = pl.DeviceIdType.MESH


def mul(a, b):
    return jnp.dot(a, b, preferred_element_type=F32)


def mul_t(a, b):
    return lax.dot_general(a, b, (((0,), (0,)), ((), ())), preferred_element_type=F32)


def kernel(
    n, snake, k1, k0, size, lags,
    anc, l_one, pat_one, l_zero, pat_zero,
    o_x0, o_x1, o_x2, tot0, tot1, tot2,
    l0_ref, l1_ref, l2_ref, acc0, acc1, acc2,
    part0, part1, part2, sib0, sib1, sib2, half0, half1, half2,
    in0, in1, in2, out0, out1, out2,
    ag_send, ag_recv, sib_send, sib_recv, pair_send, pair_recv,
    rs_send, rs_recv, fin_send, fin_recv, fs_send, fs_recv,
):
    chips = n // 2
    far = chips // 2
    rows = size
    me = lax.axis_index("row")
    core = me % 2
    chip = me // 2

    def chip_at(q):
        q = (q + chips) % chips
        if not snake:
            return q
        h = q // far
        return (1 - h) * 2 * q + h * (2 * (chips - 1 - q) + 1)

    if snake:
        y = chip % 2
        z = chip // 2
        pos = z * (1 - y) + (chips - 1 - z) * y
    else:
        pos = chip
    right = chip_at(pos + 1) * 2 + core
    left = chip_at(pos - 1) * 2 + core
    sib = chip * 2 + (1 - core)

    barrier = pltpu.get_barrier_semaphore()
    for other in (left, right, sib):
        pl.semaphore_signal(barrier, inc=1, device_id={"row": other}, device_id_type=MESH)

    groups = column_groups(k1, k0)
    bufs = (l0_ref, l1_ref, l2_ref)
    accs = (acc0, acc1, acc2)
    xouts = (o_x0, o_x1, o_x2)
    parts, sibs, halves = (part0, part1, part2), (sib0, sib1, sib2), (half0, half1, half2)
    ins, outs, tots = (in0, in1, in2), (out0, out1, out2), (tot0, tot1, tot2)

    own = pl.ds(pl.multiple_of(me * rows, rows), rows)
    for g, cols in enumerate(groups):
        for at, j in enumerate(cols):
            if j < k1:
                value = l_one[:, j * size:(j + 1) * size].astype(F32) * pat_one[0, j].astype(F32)
            else:
                j -= k1
                value = l_zero[:, j * size:(j + 1) * size].astype(F32) * pat_zero[0, j].astype(F32)
            bufs[g][own, at * size:(at + 1) * size] = value.astype(BF16)
    pl.semaphore_wait(barrier, 3)

    pending = []

    def copy(src, dst, ss, rs, target):
        return pltpu.make_async_remote_copy(
            src_ref=src, dst_ref=dst, send_sem=ss, recv_sem=rs,
            device_id={"row": target}, device_id_type=MESH)

    def start(c):
        c.start()
        pending.append(c)

    def towards(d):
        return right if d == 0 else left

    def origin(d, s):
        return pos - s if d == 0 else pos + s

    def span(d, s, count):
        cut = count // 32 * 16
        if s < far:
            return 0, count
        return (0, cut) if d == 0 else (cut, count - cut)

    def task(g):
        buf, acc, part, half, tot = bufs[g], accs[g], parts[g], halves[g], tots[g]
        hrows = part.shape[0] // 2
        piece = hrows // chips

        def gathered(view, count, send, recv, fsend, frecv):
            def ring(d, s, q):
                ref = view(q, core, *span(d, s, count))
                return copy(ref, ref, send.at[g, d, s], recv.at[g, d, s], towards(d))

            def pair(d, s, kk):
                ref = view(origin(d, s), kk, *span(d, s, count))
                return copy(ref, ref, fsend.at[g, d, s], frecv.at[g, d, s], sib)

            return ring, pair

        def block(q, kk, off, count):
            r = chip_at(q) * 2 + kk
            return buf.at[pl.ds(pl.multiple_of(r * rows + off, 16), count), :]

        def add(q, first=False):
            c = chip_at(q)
            cols = pl.ds(pl.multiple_of(c * 2 * rows, 2 * rows), 2 * rows)
            term = mul(anc[:, cols], buf[cols, :])
            if first:
                acc[...] = term
            else:
                acc[...] += term

        ring, pair = gathered(block, rows, ag_send, ag_recv, sib_send, sib_recv)
        for d in range(2):
            start(ring(d, 1, pos))
        start(pair(0, 0, core))
        yield
        for s in range(1, far + 1):
            for d in range(2):
                ring(d, s, origin(d, s)).wait_recv()
                if s < far:
                    start(ring(d, s + 1, origin(d, s)))
                start(pair(d, s, core))
            if s == 1:
                pair(0, 0, 1 - core).wait_recv()
                add(pos, True)
            else:
                for d in range(2):
                    pair(d, s - 1, 1 - core).wait_recv()
                    add(origin(d, s - 1))
            if s < far:
                yield
        for d in range(2):
            pair(d, far, 1 - core).wait_recv()
        add(pos + far)

        x = acc[...]
        xb = x.astype(BF16)
        xouts[g][...] = x.astype(xouts[g].dtype)
        own_l = jnp.concatenate([b[own, :] for b in bufs[g:]], axis=1)
        at = 0
        for i in range(len(groups[g])):
            prod = mul_t(xb[:, i * size:(i + 1) * size], own_l[:, i * size:]).astype(BF16)
            for j in range(prod.shape[1] // size):
                part[at * size:(at + 1) * size, :] = prod[:, j * size:(j + 1) * size]
                at += 1
        if at * size < part.shape[0]:
            part[at * size:, :] = jnp.zeros((part.shape[0] - at * size, size), BF16)

        def half_at(kk):
            return pl.ds(pl.multiple_of(kk * hrows, 16), hrows)

        swap = copy(part.at[half_at(1 - core), :], sibs[g], pair_send.at[g], pair_recv.at[g], sib)
        start(swap)
        yield

        swap.wait_recv()
        half[...] = part[half_at(core), :].astype(F32) + sibs[g][...].astype(F32)

        def of_piece(q):
            q = (q + chips) % chips
            return pl.ds(pl.multiple_of(q * piece, 16), piece)

        reach = (far, chips - 1 - far) if g == 0 else (chips - 1 - far, far)

        def rs(d, s):
            return copy(outs[g].at[d, s - 1], ins[g].at[d, s - 1], rs_send.at[g, d, s], rs_recv.at[g, d, s],
                        towards(d))

        for s in range(1, far + 1):
            for d in range(2):
                if s > reach[d]:
                    continue
                q = pos + (reach[d] - s + 1) * (1 if d == 0 else -1)
                value = half[of_piece(q), :]
                if s > 1:
                    rs(d, s - 1).wait_recv()
                    value = value + ins[g][d, s - 2].astype(F32)
                outs[g][d, s - 1] = value.astype(BF16)
                start(rs(d, s))
            yield
        value = half[of_piece(pos), :]
        for d in range(2):
            rs(d, reach[d]).wait_recv()
            value = value + ins[g][d, reach[d] - 1].astype(F32)
        tot[pl.ds(pl.multiple_of(core * hrows + pos * piece, 16), piece), :] = value.astype(BF16)

        def done(q, kk, off, count):
            q = (q + chips) % chips
            return tot.at[pl.ds(pl.multiple_of(kk * hrows + q * piece + off, 16), count), :]

        ring, pair = gathered(done, piece, fin_send, fin_recv, fs_send, fs_recv)
        for d in range(2):
            start(ring(d, 1, pos))
        start(pair(0, 0, core))
        yield
        for s in range(1, far + 1):
            for d in range(2):
                ring(d, s, origin(d, s)).wait_recv()
                if s < far:
                    start(ring(d, s + 1, origin(d, s)))
                start(pair(d, s, core))
            yield
        pair(0, 0, 1 - core).wait_recv()
        for s in range(1, far + 1):
            for d in range(2):
                pair(d, s, 1 - core).wait_recv()

    running = {g: task(g) for g in range(3)}
    tick = 0
    while running:
        for g in list(running):
            if tick >= lags[g] and next(running[g], "end") == "end":
                del running[g]
        tick += 1

    for c in pending:
        c.wait_send()


def column_groups(k1, k0):
    return (tuple(range(k1 // 2)), tuple(range(k1 // 2, k1)), tuple(range(k1, k1 + k0)))


def finish(
    k1, k0, size,
    x0, x1, x2, tot0, tot1, tot2, piv_one, couple, pat_couple, piv_zero,
    o_cross, o_pivot, o_low, o_couple, o_diag,
):
    where = {}
    for g, cols in enumerate(column_groups(k1, k0)):
        at = 0
        for i in cols:
            for j in range(i, k1 + k0):
                where[i, j] = (tot0, tot1, tot2)[g], at
                at += 1

    def tri(i, j):
        ref, b = where[i, j]
        return ref[b * size:(b + 1) * size, :]

    lkm = jnp.concatenate([
        jnp.concatenate([
            (couple[i * size:(i + 1) * size, j * size:(j + 1) * size].astype(F32)
             * jnp.broadcast_to(pat_couple[i:i + 1, j:j + 1].astype(F32), (size, size))).astype(BF16)
            for j in range(k0)], axis=1) for i in range(k1)], axis=0)

    for i in range(k1):
        for j in range(i, k1):
            g = tri(i, j).astype(F32)
            ri, rj = slice(i * size, (i + 1) * size), slice(j * size, (j + 1) * size)
            if i == j:
                o_pivot[ri, rj] = g + piv_one[ri, :]
            else:
                o_pivot[ri, rj] = g
                o_pivot[rj, ri] = g.T
    xb = jnp.concatenate([x0[...], x1[...]], axis=1)
    o_cross[...] = -xb
    o_low[...] = (mul(xb, lkm) - x2[...]).astype(BF16)
    pivot_b = o_pivot[...].astype(BF16)
    cross = jnp.concatenate(
        [jnp.concatenate([tri(i, k1 + j) for j in range(k0)], axis=1) for i in range(k1)], axis=0)
    coupled = cross.astype(F32) - mul(pivot_b, lkm)
    o_couple[...] = coupled
    high = coupled.astype(BF16)
    low = (coupled - high.astype(F32)).astype(BF16)
    update = mul_t(cross, lkm) + mul_t(lkm, high) + mul_t(lkm, low)
    for i in range(k0):
        for j in range(i, k0):
            g = tri(k1 + i, k1 + j).astype(F32)
            ri, rj = slice(i * size, (i + 1) * size), slice(j * size, (j + 1) * size)
            if i == j:
                o_diag[ri, rj] = g + piv_zero[ri, :] - update[ri, rj]
            else:
                o_diag[ri, rj] = g - update[ri, rj]
                o_diag[rj, ri] = g.T - update[rj, ri]


LAGS = (0, 1, 2)


def per_device(n, snake, *args):
    anc, l_one, pat_one, piv_one, l_zero, pat_zero, couple, pat_couple, piv_zero = args
    rows, order = anc.shape
    size = piv_one.shape[1]
    w1, w0 = l_one.shape[1], l_zero.shape[1]
    k1, k0 = w1 // size, w0 // size
    far = n // 4
    groups = column_groups(k1, k0)
    widths = [len(g) * size for g in groups]
    unit = 16 * n
    packed = [-(-sum(k1 + k0 - i for i in g) * size // unit) * unit for g in groups]
    vmem = pl.BlockSpec(memory_space=pltpu.VMEM)
    smem = pl.BlockSpec(memory_space=pltpu.SMEM)
    dma = pltpu.SemaphoreType.DMA
    steps = dma((3, 2, far + 1))
    limit = 56 * 1024 * 1024
    sums = pl.pallas_call(
        functools.partial(kernel, n, snake, k1, k0, size, LAGS),
        out_shape=(
            jax.ShapeDtypeStruct((rows, widths[0]), BF16),
            jax.ShapeDtypeStruct((rows, widths[1]), BF16),
            jax.ShapeDtypeStruct((rows, widths[2]), F32),
            *(jax.ShapeDtypeStruct((p, size), BF16) for p in packed),
        ),
        in_specs=[vmem, vmem, smem, vmem, smem],
        out_specs=(vmem,) * 6,
        scratch_shapes=[
            *(pltpu.VMEM((order, w), BF16) for w in widths),
            *(pltpu.VMEM((rows, w), F32) for w in widths),
            *(pltpu.VMEM((p, size), BF16) for p in packed),
            *(pltpu.VMEM((p // 2, size), BF16) for p in packed),
            *(pltpu.VMEM((p // 2, size), F32) for p in packed),
            *(pltpu.VMEM((2, far, p // n, size), BF16) for p in packed),
            *(pltpu.VMEM((2, far, p // n, size), BF16) for p in packed),
            steps, steps, steps, steps,
            dma((3,)), dma((3,)),
            steps, steps, steps, steps, steps, steps,
        ],
        compiler_params=pltpu.CompilerParams(
            collective_id=0, has_side_effects=True, vmem_limit_bytes=limit),
    )(anc, l_one, pat_one, l_zero, pat_zero)
    return pl.pallas_call(
        functools.partial(finish, k1, k0, size),
        out_shape=(
            jax.ShapeDtypeStruct((rows, w1), BF16),
            jax.ShapeDtypeStruct((w1, w1), F32),
            jax.ShapeDtypeStruct((rows, w0), BF16),
            jax.ShapeDtypeStruct((w1, w0), F32),
            jax.ShapeDtypeStruct((w0, w0), F32),
        ),
        in_specs=[vmem] * 10,
        out_specs=(vmem,) * 5,
        compiler_params=pltpu.CompilerParams(vmem_limit_bytes=limit),
    )(*sums, piv_one, couple, pat_couple, piv_zero)


def solution(mesh):
    n = mesh.shape["row"]
    placed = (
        P(("pole", "row"), None),
        P(("pole", "row"), None),
        P("row", None),
        P("pole", None),
        P(("pole", "row"), None),
        P("row", None),
        P("pole", None),
        P(),
        P("pole", None),
    )
    return jax.shard_map(
        functools.partial(per_device, n, n == 16),
        mesh=mesh,
        in_specs=placed,
        out_specs=(
            P(("pole", "row"), None),
            P("pole", None),
            P(("pole", "row"), None),
            P("pole", None),
            P("pole", None),
        ),
        check_vma=False,
    )
```
